32 devices in a mesh: dp: 16 (over z, y, x), tensor: 2 (over core).
Axes of the slice: x: 2, y: 2, z: 4, core: 2. Of those that a mesh axis runs over, the one named last changes fastest.
Arguments:
- inputs: bfloat16 [8192, 768], P(('dp', 'tensor')), may hold values from -8 to 8
- segments: int32 [16, 512], P('dp'), may hold values from 0 to 3, as said below
- norm_gains: float32 [2, 768], replicated, may hold values from 0.1 to 1.9
- norm_shifts: float32 [2, 768], replicated, may hold values from -3 to 3
- qkv_weight: bfloat16 [3, 768, 768], P(None, 'dp', 'tensor'), may hold values from -2 to 2
- qkv_bias: float32 [2, 768], P(None, 'tensor'), may hold values from -3 to 3
- out_weight: bfloat16 [768, 768], P('tensor', 'dp'), may hold values from -1.75 to 1.75
- out_biases: float32 [2, 768], replicated, may hold values from -3 to 3
- up_weight: bfloat16 [768, 3072], P('dp', 'tensor'), may hold values from -0.21875 to 0.21875
- up_bias: float32 [3072], P('tensor'), may hold values from -3 to 3
- down_weight: bfloat16 [3072, 768], P('tensor', 'dp'), may hold values from -0.109375 to 0.109375
- cotangent: bfloat16 [8192, 768], P(('dp', 'tensor')), may hold values from -6 to 6
Outputs:
- output: bfloat16 [8192, 768], P(('dp', 'tensor'))
- input_grad: float32 [8192, 768], P(('dp', 'tensor'))
- norm_gains_grad: float32 [2, 768], replicated
- norm_shifts_grad: float32 [2, 768], replicated
- qkv_weight_grad: float32 [3, 768, 768], P(None, 'dp', 'tensor')
- qkv_bias_grad: float32 [2, 768], P(None, 'tensor')
- out_weight_grad: float32 [768, 768], P('tensor', 'dp')
- out_biases_grad: float32 [2, 768], replicated
- up_weight_grad: float32 [768, 3072], P('dp', 'tensor')
- up_bias_grad: float32 [3072], P('tensor')
- down_weight_grad: float32 [3072, 768], P('tensor', 'dp')
The draws below stay inside these ranges and needn't reach their ends.
Inputs may be any that keep to these rules, and one draw needn't show every extreme that they name: `segments`: within each sequence of 512 tokens the segment numbers start at 0 and never fall; each rise marks the start of another document.
All inputs are finite; a program needn't handle non-finite values.
Results may differ from the reference program's by a relative error of at most 0.012.
The reference program's roundings to bfloat16 on the way count: a program that leaves them out, or rounds other values in their place, can miss the bound.
Values may be sent and summed in bfloat16 or wider, within the bound.
A program may use at most 128 MiB of HBM per device.

```python
import math
import jax
import jax.numpy as jnp
from jax import lax

D = 768
HEADS = 12
HEAD = 64
FF = 3072
SEQ = 512
SEQS = 16
TOKENS = 8192


def draw_inputs(key, part):
    key_one = jax.random.fold_in(key, 0)
    drawn = jax.random.normal(key_one, (TOKENS, D), jnp.float32)
    return jnp.clip(drawn, -8.0, 8.0).astype(jnp.bfloat16)


def draw_segments(key, part):
    shortest = SEQ * 200 // 512
    longest = SEQ * 2000 // 512
    doc_count = TOKENS // shortest + 4
    key_one, key_two = jax.random.split(jax.random.fold_in(key, 7))
    doc_lengths = jax.random.randint(key_one, (doc_count,), shortest, longest + 1, dtype=jnp.int32)
    leading = jax.random.randint(key_two, (), 1, SEQ - 2 * shortest, dtype=jnp.int32)
    doc_lengths = doc_lengths.at[0].set(leading).at[1].set(shortest).at[2].set(shortest)
    doc_ends = jnp.cumsum(doc_lengths).astype(jnp.int32)
    places = jnp.arange(TOKENS, dtype=jnp.int32)
    owners = jnp.searchsorted(doc_ends, places, side='right').astype(jnp.int32)
    grouped = owners.reshape(SEQS, SEQ)
    return (grouped - grouped[:, :1]).astype(jnp.int32)


def draw_qkv_weight(key, part):
    key_one = jax.random.fold_in(key, 3)
    drawn = jax.random.normal(key_one, (3, D, D), jnp.float32) / math.sqrt(D)
    return jnp.clip(drawn, -2.0, 2.0).astype(jnp.bfloat16)


def strengthened(values, key, source, target, shards_of, factor):
    def block_of(axis_at):
        return (jnp.arange(values.shape[axis_at]) // (values.shape[axis_at] // shards_of)).reshape((-1,) + (1,) * (values.ndim - 1 - axis_at))

    first = jax.random.permutation(key, shards_of)[block_of(target)]
    other_side = (block_of(target) + shards_of // 2) % shards_of
    return jnp.where((block_of(source) == first) | (block_of(source) == other_side), factor * values, values)


def steps_of(stream_key, shape, pieces, low, high):
    level = 1.0
    for axis_at, blocks in pieces:
        steps = jax.random.uniform(jax.random.fold_in(jax.random.fold_in(stream_key, 6), axis_at), (blocks,), jnp.float32, low / len(pieces), high / len(pieces))
        level = level * jnp.repeat(jnp.exp(steps), shape[axis_at] // blocks).reshape((-1,) + (1,) * (len(shape) - 1 - axis_at))
    return level


def centred(key, dims, scale, limit, pieces=(), held_as=jnp.bfloat16):
    entries = jax.random.normal(key, dims, jnp.float32) * scale
    if len(pieces) > 0:
        entries = steps_of(key, dims, pieces, -0.22, 0.18) * entries
    return jnp.clip(entries, min=-limit, max=limit).astype(held_as)


def noise_with(stream_key, extent, scale, limit, cuts, heavy, held_as=jnp.bfloat16):
    entries = scale * jax.random.normal(stream_key, extent, jnp.float32)
    if cuts:
        entries = entries * steps_of(stream_key, extent, cuts, -0.22, 0.18)
    return jnp.clip(strengthened(entries, jax.random.fold_in(stream_key, 3), *heavy), -limit, limit).astype(held_as)


def setup_inputs(seed: int = 0) -> dict:
    splits = jax.random.split(jax.random.key(seed), 13)
    inputs = draw_inputs(jax.random.fold_in(splits[12], 71), 0)
    segments = draw_segments(jax.random.fold_in(splits[12], 71), 0)
    norm_gains = jnp.clip(1.0 + 0.18 * jax.random.normal(splits[2], (2, D), jnp.float32), 0.1, 1.9)
    norm_shifts = centred(splits[3], (2, D), 0.5, 3.0, (), jnp.float32)
    qkv_weight = draw_qkv_weight(jax.random.fold_in(splits[12], 71), 0)
    qkv_bias = centred(splits[5], (2, D), 0.5, 3.0, ((1, 2),), jnp.float32)
    out_weight = centred(splits[6], (D, D), (D // 64) ** -0.5, 1.75, ((0, 2), (1, 16)))
    out_biases = centred(splits[7], (2, D), 0.5, 3.0, (), jnp.float32)
    up_weight = centred(splits[8], (D, FF), D ** -0.5, 0.21875, ((0, 16), (1, 2)))
    up_bias = centred(splits[9], (FF,), 0.5, 3.0, ((0, 2),), jnp.float32)
    down_weight = centred(splits[10], (FF, D), FF ** -0.5, 0.109375, ((0, 2), (1, 16)))
    cotangent = noise_with(splits[11], (TOKENS, D), 1.0, 6.0, ((0, 32),), (0, 1, 32, 2.75))
    return {"inputs": inputs, "segments": segments, "norm_gains": norm_gains, "norm_shifts": norm_shifts, "qkv_weight": qkv_weight, "qkv_bias": qkv_bias, "out_weight": out_weight, "out_biases": out_biases, "up_weight": up_weight, "up_bias": up_bias, "down_weight": down_weight, "cotangent": cotangent}


EPSILON = 1e-05
MASKED = -1e+30

def normalize(row_block, gain, shift):
    center = lax.optimization_barrier(jnp.mean(row_block, axis=-1, keepdims=True))
    centered = row_block - center
    spread = lax.optimization_barrier(jnp.mean(centered * centered, axis=-1, keepdims=True))
    inverse = lax.rsqrt(spread + EPSILON)
    unit_rows = centered * inverse
    return (unit_rows * gain + shift, unit_rows, inverse)

def normalize_back(grad_rows, unit_rows, inverse, gain):
    scaled = grad_rows * gain
    first_mean = lax.optimization_barrier(jnp.mean(scaled, axis=-1, keepdims=True))
    second_mean = lax.optimization_barrier(jnp.mean(scaled * unit_rows, axis=-1, keepdims=True))
    return inverse * (scaled - first_mean - unit_rows * second_mean)

def gaussian_unit(values_in):
    return jax.nn.gelu(values_in, approximate=True)

def as_wide(narrow):
    return lax.optimization_barrier(narrow).astype(jnp.float32)

def allowed_pairs(segment_ids):
    length = segment_ids.shape[0]
    places = jnp.arange(length)
    return (segment_ids[:, None] == segment_ids[None, :]) & (places[:, None] >= places[None, :])

def attention_scores(queries, keys_in, allowed):
    scores = jnp.einsum('qhd,khd->hqk', as_wide(queries), as_wide(keys_in)) * HEAD ** (-0.5)
    return jnp.where(allowed[None], scores, MASKED)

def attend(queries, keys_in, values_in, allowed):
    scores = attention_scores(queries, keys_in, allowed)
    row_top = lax.optimization_barrier(jnp.max(scores, axis=-1, keepdims=True))
    log_total = row_top + jnp.log(lax.optimization_barrier(jnp.sum(jnp.exp(scores - row_top), axis=-1, keepdims=True)))
    soft_weights = jnp.exp(scores - log_total).astype(jnp.bfloat16)
    mixed = jnp.einsum('hqk,khd->qhd', as_wide(soft_weights), as_wide(values_in))
    return (mixed.astype(jnp.bfloat16), log_total)

def attend_back(queries, keys_in, values_in, allowed, log_total, grad_mixed):
    scores = attention_scores(queries, keys_in, allowed)
    probs = jnp.exp(scores - log_total)
    soft_weights = probs.astype(jnp.bfloat16)
    grad_values = jnp.einsum('hqk,qhd->khd', as_wide(soft_weights), as_wide(grad_mixed))
    grad_probs = jnp.einsum('qhd,khd->hqk', as_wide(grad_mixed), as_wide(values_in))
    row_dot = lax.optimization_barrier(jnp.sum(probs * grad_probs, axis=-1, keepdims=True))
    grad_scores = (probs * (grad_probs - row_dot) * HEAD ** (-0.5)).astype(jnp.bfloat16)
    grad_queries = jnp.einsum('hqk,khd->qhd', as_wide(grad_scores), as_wide(keys_in))
    grad_keys = jnp.einsum('hqk,qhd->khd', as_wide(grad_scores), as_wide(queries))
    return (grad_queries, grad_keys, grad_values)

def layer_pass(params, sequence_in, segment_ids, grad_out):
    norm_gains, norm_shifts, qkv_weight, qkv_bias, out_weight, out_biases, up_weight, up_bias, down_weight = params
    length = sequence_in.shape[0]
    allowed = allowed_pairs(segment_ids)
    stream = sequence_in.astype(jnp.float32)
    normed, unit_one, inverse_one = normalize(stream, norm_gains[0], norm_shifts[0])
    hidden_one = normed.astype(jnp.bfloat16)
    queries = (jnp.dot(hidden_one, qkv_weight[0], preferred_element_type=jnp.float32) + qkv_bias[0]).astype(jnp.bfloat16).reshape(length, HEADS, HEAD)
    keys_in = jnp.dot(hidden_one, qkv_weight[1], preferred_element_type=jnp.float32).astype(jnp.bfloat16).reshape(length, HEADS, HEAD)
    values_in = (jnp.dot(hidden_one, qkv_weight[2], preferred_element_type=jnp.float32) + qkv_bias[1]).astype(jnp.bfloat16).reshape(length, HEADS, HEAD)
    mixed, log_total = attend(queries, keys_in, values_in, allowed)
    mixed_rows = mixed.reshape(length, D)
    middle = stream + jnp.dot(mixed_rows, out_weight, preferred_element_type=jnp.float32) + out_biases[0]
    normed_two, unit_two, inverse_two = normalize(middle, norm_gains[1], norm_shifts[1])
    hidden_two = normed_two.astype(jnp.bfloat16)
    before = jnp.dot(hidden_two, up_weight, preferred_element_type=jnp.float32) + up_bias
    activated = gaussian_unit(before).astype(jnp.bfloat16)
    result = (middle + jnp.dot(activated, down_weight, preferred_element_type=jnp.float32) + out_biases[1]).astype(jnp.bfloat16)
    grad_stream = grad_out.astype(jnp.float32)
    grad_down = jnp.dot(activated.T, grad_out, preferred_element_type=jnp.float32)
    grad_active = jnp.dot(grad_out, down_weight.T, preferred_element_type=jnp.float32)
    grad_before = jax.vjp(gaussian_unit, before)[1](grad_active)[0]
    before_low = grad_before.astype(jnp.bfloat16)
    grad_up = jnp.dot(hidden_two.T, before_low, preferred_element_type=jnp.float32)
    grad_hidden_two = jnp.dot(before_low, up_weight.T, preferred_element_type=jnp.float32)
    grad_middle = grad_stream + normalize_back(grad_hidden_two, unit_two, inverse_two, norm_gains[1])
    middle_low = grad_middle.astype(jnp.bfloat16)
    grad_outw = jnp.dot(mixed_rows.T, middle_low, preferred_element_type=jnp.float32)
    grad_mixed = jnp.dot(middle_low, out_weight.T, preferred_element_type=jnp.float32).astype(jnp.bfloat16).reshape(length, HEADS, HEAD)
    grad_queries, grad_keys, grad_values = attend_back(queries, keys_in, values_in, allowed, log_total, grad_mixed)
    grad_stack = jnp.stack([grad_queries.reshape(length, D), grad_keys.reshape(length, D), grad_values.reshape(length, D)])
    stack_low = grad_stack.astype(jnp.bfloat16)
    grad_qkv = jnp.stack([jnp.dot(hidden_one.T, stack_low[0], preferred_element_type=jnp.float32), jnp.dot(hidden_one.T, stack_low[1], preferred_element_type=jnp.float32), jnp.dot(hidden_one.T, stack_low[2], preferred_element_type=jnp.float32)])
    grad_hidden_one = jnp.dot(stack_low[0], qkv_weight[0].T, preferred_element_type=jnp.float32) + jnp.dot(stack_low[1], qkv_weight[1].T, preferred_element_type=jnp.float32) + jnp.dot(stack_low[2], qkv_weight[2].T, preferred_element_type=jnp.float32)
    grad_input = grad_middle + normalize_back(grad_hidden_one, unit_one, inverse_one, norm_gains[0])
    vectors = jnp.stack([lax.optimization_barrier(jnp.sum(grad_hidden_one * unit_one, axis=0)), lax.optimization_barrier(jnp.sum(grad_hidden_two * unit_two, axis=0)), lax.optimization_barrier(jnp.sum(grad_hidden_one, axis=0)), lax.optimization_barrier(jnp.sum(grad_hidden_two, axis=0)), lax.optimization_barrier(jnp.sum(grad_middle, axis=0)), lax.optimization_barrier(jnp.sum(grad_stream, axis=0))])
    bias_grad = jnp.stack([lax.optimization_barrier(jnp.sum(grad_stack[0], axis=0)), lax.optimization_barrier(jnp.sum(grad_stack[2], axis=0))])
    hidden_bias = lax.optimization_barrier(jnp.sum(grad_before, axis=0))
    return (result, grad_input, (vectors, grad_qkv, bias_grad, grad_outw, grad_up, hidden_bias, grad_down))

def reference(inputs, segments, norm_gains, norm_shifts, qkv_weight, qkv_bias, out_weight, out_biases, up_weight, up_bias, down_weight, cotangent):
    params = (norm_gains, norm_shifts, qkv_weight, qkv_bias, out_weight, out_biases, up_weight, up_bias, down_weight)
    grouped = (inputs.reshape(SEQS, SEQ, D), segments, cotangent.reshape(SEQS, SEQ, D))
    totals = (jnp.zeros((6, D), jnp.float32), jnp.zeros((3, D, D), jnp.float32), jnp.zeros((2, D), jnp.float32), jnp.zeros((D, D), jnp.float32), jnp.zeros((D, FF), jnp.float32), jnp.zeros((FF,), jnp.float32), jnp.zeros((FF, D), jnp.float32))

    def advance(running, seq_piece):
        result, grad_input, grads = layer_pass(params, seq_piece[0], seq_piece[1], seq_piece[2])
        summed = jax.tree.map(lambda held, adding: held + adding, running, grads)
        return (summed, (result, grad_input))
    totals, (results, grad_inputs) = lax.scan(advance, totals, grouped)
    vectors, grad_qkv, bias_grad, grad_outw, grad_up, hidden_bias, grad_down = totals
    return (results.reshape(TOKENS, D), grad_inputs.reshape(TOKENS, D), vectors[0:2], vectors[2:4], grad_qkv, bias_grad, grad_outw, vectors[4:6], grad_up, hidden_bias, grad_down)
```

```python
import jax
import jax.numpy as jnp
from jax import lax
from jax.sharding import PartitionSpec as P

HEAD = 64


EPSILON = 1e-05
MASKED = -1e30


def normalize(row_block, gain, shift):
    center = jnp.mean(row_block, axis=-1, keepdims=True)
    centered = row_block - center
    spread = jnp.mean(centered * centered, axis=-1, keepdims=True)
    inverse = lax.rsqrt(spread + EPSILON)
    unit_rows = centered * inverse
    return (unit_rows * gain + shift, unit_rows, inverse)


def normalize_back(grad_rows, unit_rows, inverse, gain):
    scaled = grad_rows * gain
    first_mean = jnp.mean(scaled, axis=-1, keepdims=True)
    second_mean = jnp.mean(scaled * unit_rows, axis=-1, keepdims=True)
    return inverse * (scaled - first_mean - unit_rows * second_mean)


def gaussian_unit(values_in):
    return jax.nn.gelu(values_in, approximate=True)


def allowed_pairs(segment_ids):
    length = segment_ids.shape[0]
    places = jnp.arange(length)
    return (segment_ids[:, None] == segment_ids[None, :]) & (places[:, None] >= places[None, :])


def attention_scores(queries, keys_in, allowed):
    scores = jnp.einsum(
        "qhd,khd->hqk", queries, keys_in, preferred_element_type=jnp.float32
    ) * HEAD ** (-0.5)
    return jnp.where(allowed[None], scores, MASKED)


def attend(packed):
    queries, keys_in, values_in, segment_ids = packed
    allowed = allowed_pairs(segment_ids)
    scores = attention_scores(queries, keys_in, allowed)
    row_top = jnp.max(scores, axis=-1, keepdims=True)
    log_total = row_top + jnp.log(jnp.sum(jnp.exp(scores - row_top), axis=-1, keepdims=True))
    soft_weights = jnp.exp(scores - log_total).astype(jnp.bfloat16)
    mixed = jnp.einsum("hqk,khd->qhd", soft_weights, values_in, preferred_element_type=jnp.float32)
    return (mixed.astype(jnp.bfloat16), log_total)


def attend_back(packed):
    queries, keys_in, values_in, segment_ids, log_total, grad_mixed = packed
    allowed = allowed_pairs(segment_ids)
    scores = attention_scores(queries, keys_in, allowed)
    probs = jnp.exp(scores - log_total)
    soft_weights = probs.astype(jnp.bfloat16)
    grad_values = jnp.einsum(
        "hqk,qhd->khd", soft_weights, grad_mixed, preferred_element_type=jnp.float32
    )
    grad_probs = jnp.einsum(
        "qhd,khd->hqk", grad_mixed, values_in, preferred_element_type=jnp.float32
    )
    row_dot = jnp.sum(probs * grad_probs, axis=-1, keepdims=True)
    grad_scores = (probs * (grad_probs - row_dot) * HEAD ** (-0.5)).astype(jnp.bfloat16)
    grad_queries = jnp.einsum(
        "hqk,khd->qhd", grad_scores, keys_in, preferred_element_type=jnp.float32
    )
    grad_keys = jnp.einsum("hqk,qhd->khd", grad_scores, queries, preferred_element_type=jnp.float32)
    return (grad_queries, grad_keys, grad_values)


def partner_pairs(count, step):
    return [(place, place ^ step) for place in range(count)]


def bit_shape(bit_count):
    return (2,) * bit_count


def gather_rows(shard, order, data_rank, data_count, bit_count):
    rows, cols = shard.shape
    mine = [(data_rank >> (bit_count - 1 - place)) & 1 for place in range(bit_count)]
    zero = jnp.int32(0)
    held = jnp.zeros(bit_shape(bit_count) + (rows, cols), shard.dtype)
    piece = shard.reshape((1,) * bit_count + (rows, cols))
    held = lax.dynamic_update_slice(held, piece, mine + [zero, zero])
    done = []
    for bit in order:
        place = bit_count - 1 - bit
        arrived = lax.ppermute(piece, "dp", partner_pairs(data_count, 1 << bit))
        target = [zero if at in done else mine[at] for at in range(bit_count)]
        target[place] = 1 - mine[place]
        held = lax.dynamic_update_slice(held, arrived, target + [zero, zero])
        done.append(place)
        if len(done) < bit_count:
            starts = [zero if at in done else mine[at] for at in range(bit_count)]
            sizes = [2 if at in done else 1 for at in range(bit_count)]
            piece = lax.dynamic_slice(held, starts + [zero, zero], sizes + [rows, cols])
    return held.reshape(data_count * rows, cols)


def scatter_sum(term, order, data_rank, data_count, bit_count):
    rows, cols = term.shape[0] // data_count, term.shape[1]
    mine = [(data_rank >> (bit_count - 1 - place)) & 1 for place in range(bit_count)]
    held = term.reshape(bit_shape(bit_count) + (rows, cols))
    for bit in order:
        place = bit_count - 1 - bit
        away = lax.dynamic_slice_in_dim(held, 1 - mine[place], 1, place).astype(jnp.bfloat16)
        kept = lax.dynamic_slice_in_dim(held, mine[place], 1, place)
        arrived = lax.ppermute(away, "dp", partner_pairs(data_count, 1 << bit))
        held = kept + arrived.astype(jnp.float32)
    return held.reshape(rows, cols)


def total_over(flat, data_count, bit_count):
    for bit in range(bit_count):
        flat = flat + lax.ppermute(flat, "dp", partner_pairs(data_count, 1 << bit))
    return flat


def local(
    inputs,
    segments,
    norm_gains,
    norm_shifts,
    qkv_weight,
    qkv_bias,
    out_weight,
    out_biases,
    up_weight,
    up_bias,
    down_weight,
    cotangent,
):
    local_rows = inputs.shape[0]
    seq_count = segments.shape[0]
    seq_length = segments.shape[1]
    model_width = inputs.shape[1]
    tensor_rank = lax.axis_index("tensor")
    data_rank = lax.axis_index("dp")
    data_count = lax.axis_size("dp")
    bit_count = data_count.bit_length() - 1
    head_cols = qkv_weight.shape[2]
    hidden_cols = up_weight.shape[1]
    heads_here = head_cols // HEAD
    block_rows = seq_count * seq_length
    links = (data_rank, data_count, bit_count)
    rest = [bit for bit in range(bit_count - 1, 2, -1)]
    order_up = rest + [2, 1, 0]
    order_down = rest + [2, 0, 1]
    order_qkv = rest + [1, 0, 2]

    first = jnp.concatenate([qkv_weight[0], qkv_weight[1], qkv_weight[2], out_weight.T], axis=1)
    first_full = gather_rows(first, order_qkv, *links)
    up_full = gather_rows(up_weight, order_up, *links)
    down_full = gather_rows(down_weight.T, order_down, *links)
    qkv_full = first_full[:, : 3 * head_cols]
    out_full = first_full[:, 3 * head_cols :]

    def spread(row_block):
        return lax.all_gather(row_block, "tensor", axis=0, tiled=True)

    def collect(left_rows, right_matrix, dims):
        def term(rank):
            part = lax.dynamic_slice_in_dim(left_rows, rank * local_rows, local_rows, 0)
            return lax.dot_general(
                part, right_matrix, (dims, ((), ())), preferred_element_type=jnp.float32
            )

        arrived = lax.ppermute(term(1 - tensor_rank), "tensor", [(0, 1), (1, 0)])
        return term(tensor_rank) + arrived

    plain, turned = ((1,), (0,)), ((1,), (1,))
    stream = inputs.astype(jnp.float32)
    normed, unit_one, inverse_one = normalize(stream, norm_gains[0], norm_shifts[0])
    hidden_one = spread(normed.astype(jnp.bfloat16))
    grad_stream = cotangent.astype(jnp.float32)
    grad_rows = spread(cotangent)
    projected = jnp.dot(hidden_one, qkv_full, preferred_element_type=jnp.float32)
    head_shape = (seq_count, seq_length, heads_here, HEAD)
    queries = (projected[:, :head_cols] + qkv_bias[0]).astype(jnp.bfloat16).reshape(head_shape)
    keys_in = projected[:, head_cols : 2 * head_cols].astype(jnp.bfloat16).reshape(head_shape)
    values_in = (
        (projected[:, 2 * head_cols :] + qkv_bias[1]).astype(jnp.bfloat16).reshape(head_shape)
    )
    mixed, log_total = lax.map(attend, (queries, keys_in, values_in, segments))
    mixed_rows = mixed.reshape(block_rows, head_cols)
    middle = stream + collect(mixed_rows, out_full, turned) + out_biases[0]
    normed_two, unit_two, inverse_two = normalize(middle, norm_gains[1], norm_shifts[1])
    hidden_two = spread(normed_two.astype(jnp.bfloat16))
    before = jnp.dot(hidden_two, up_full, preferred_element_type=jnp.float32) + up_bias
    activated = gaussian_unit(before).astype(jnp.bfloat16)
    down_turned = jnp.einsum("rd,rj->dj", grad_rows, activated, preferred_element_type=jnp.float32)
    down_summed = scatter_sum(down_turned, order_down[::-1], *links).T
    grad_active = jnp.dot(grad_rows, down_full, preferred_element_type=jnp.float32)
    grad_before = jax.vjp(gaussian_unit, before)[1](grad_active)[0]
    before_low = grad_before.astype(jnp.bfloat16)
    grad_up = jnp.einsum("rd,rj->dj", hidden_two, before_low, preferred_element_type=jnp.float32)
    up_summed = scatter_sum(grad_up, order_up[::-1], *links)
    grad_hidden_two = collect(before_low, up_full, turned)
    grad_middle = grad_stream + normalize_back(
        grad_hidden_two, unit_two, inverse_two, norm_gains[1]
    )
    middle_rows = spread(grad_middle.astype(jnp.bfloat16))
    out_turned = jnp.einsum(
        "rd,rj->dj", middle_rows, mixed_rows, preferred_element_type=jnp.float32
    )
    grad_mixed = (
        jnp.dot(middle_rows, out_full, preferred_element_type=jnp.float32)
        .astype(jnp.bfloat16)
        .reshape(head_shape)
    )
    result = (middle + collect(activated, down_full, turned) + out_biases[1]).astype(jnp.bfloat16)
    grad_queries, grad_keys, grad_values = lax.map(
        attend_back, (queries, keys_in, values_in, segments, log_total, grad_mixed)
    )
    grad_queries = grad_queries.reshape(block_rows, head_cols)
    grad_keys = grad_keys.reshape(block_rows, head_cols)
    grad_values = grad_values.reshape(block_rows, head_cols)
    stack_low = jnp.concatenate([grad_queries, grad_keys, grad_values], axis=1).astype(jnp.bfloat16)
    grad_qkv = jnp.einsum("rd,rj->dj", hidden_one, stack_low, preferred_element_type=jnp.float32)
    first_summed = scatter_sum(
        jnp.concatenate([grad_qkv, out_turned], axis=1), order_qkv[::-1], *links
    )
    qkv_summed = jnp.stack(
        [first_summed[:, at * head_cols : (at + 1) * head_cols] for at in range(3)]
    )
    out_summed = first_summed[:, 3 * head_cols :].T
    grad_hidden_one = collect(stack_low, qkv_full, turned)
    grad_input = grad_middle + normalize_back(grad_hidden_one, unit_one, inverse_one, norm_gains[0])
    vectors = jnp.concatenate(
        [
            jnp.sum(grad_hidden_one * unit_one, axis=0),
            jnp.sum(grad_hidden_two * unit_two, axis=0),
            jnp.sum(grad_hidden_one, axis=0),
            jnp.sum(grad_hidden_two, axis=0),
            jnp.sum(grad_middle, axis=0),
            jnp.sum(grad_stream, axis=0),
        ]
    )
    vectors = vectors + lax.ppermute(vectors, "tensor", [(0, 1), (1, 0)])
    flat = jnp.concatenate(
        [
            vectors,
            jnp.sum(grad_queries, axis=0),
            jnp.sum(grad_values, axis=0),
            jnp.sum(grad_before, axis=0),
        ]
    )
    flat = total_over(flat, data_count, bit_count)
    vector_total = flat[: 6 * model_width].reshape(6, model_width)
    rest_total = flat[6 * model_width :]
    qkv_bias_grad = rest_total[: 2 * head_cols].reshape(2, head_cols)
    up_bias_grad = rest_total[2 * head_cols :]
    return (
        result,
        grad_input,
        vector_total[0:2],
        vector_total[2:4],
        qkv_summed,
        qkv_bias_grad,
        out_summed,
        vector_total[4:6],
        up_summed,
        up_bias_grad,
        down_summed,
    )


def solution(mesh):
    in_specs = (
        P(("dp", "tensor"), None),
        P("dp", None),
        P(),
        P(),
        P(None, "dp", "tensor"),
        P(None, "tensor"),
        P("tensor", "dp"),
        P(),
        P("dp", "tensor"),
        P("tensor"),
        P("tensor", "dp"),
        P(("dp", "tensor"), None),
    )
    out_specs = (
        P(("dp", "tensor"), None),
        P(("dp", "tensor"), None),
        P(),
        P(),
        P(None, "dp", "tensor"),
        P(None, "tensor"),
        P("tensor", "dp"),
        P(),
        P("dp", "tensor"),
        P("tensor"),
        P("tensor", "dp"),
    )
    return jax.shard_map(local, mesh=mesh, in_specs=in_specs, out_specs=out_specs, check_vma=False)
```

```python
import jax
import jax.numpy as jnp
from jax import lax
from jax.experimental import pallas as pl
from jax.experimental.pallas import tpu as pltpu
from jax.sharding import PartitionSpec as P

HEAD = 64


EPSILON = 1e-05
MASKED = -1e30


def normalize(row_block, gain, shift):
    center = jnp.mean(row_block, axis=-1, keepdims=True)
    centered = row_block - center
    spread = jnp.mean(centered * centered, axis=-1, keepdims=True)
    inverse = lax.rsqrt(spread + EPSILON)
    unit_rows = centered * inverse
    return (unit_rows * gain + shift, unit_rows, inverse)


def normalize_back(grad_rows, unit_rows, inverse, gain):
    scaled = grad_rows * gain
    first_mean = jnp.mean(scaled, axis=-1, keepdims=True)
    second_mean = jnp.mean(scaled * unit_rows, axis=-1, keepdims=True)
    return inverse * (scaled - first_mean - unit_rows * second_mean)


def gaussian_unit(values_in):
    return jax.nn.gelu(values_in, approximate=True)


def dot(left, right, left_dim, right_dim):
    return lax.dot_general(
        left, right, (((left_dim,), (right_dim,)), ((), ())), preferred_element_type=jnp.float32
    )


def allowed_block(seg_column, seg_row, start, rows, span):
    row_at = lax.broadcasted_iota(jnp.int32, (rows, span), 0) + start
    col_at = lax.broadcasted_iota(jnp.int32, (rows, span), 1)
    same = seg_column[start : start + rows, :] == seg_row[:, :span]
    return same & (row_at >= col_at)


def attend_kernel(stack_ref, seg_column_ref, seg_row_ref, mixed_ref, log_ref):
    length, width = mixed_ref.shape
    heads = width // HEAD
    rows = length // 2
    seg_column, seg_row = seg_column_ref[...], seg_row_ref[0]
    for block in range(2):
        start, span = block * rows, (block + 1) * rows
        allowed = allowed_block(seg_column, seg_row, start, rows, span)
        for head in range(heads):
            at = head * HEAD
            queries = stack_ref[start:span, at : at + HEAD]
            keys_in = stack_ref[:span, width + at : width + at + HEAD]
            values_in = stack_ref[:span, 2 * width + at : 2 * width + at + HEAD]
            scores = jnp.where(allowed, dot(queries, keys_in, 1, 1) * HEAD ** (-0.5), MASKED)
            top = jnp.max(scores, axis=-1, keepdims=True)
            total = jnp.sum(jnp.exp(scores - top), axis=-1, keepdims=True)
            log_total = top + jnp.log(total)
            soft = jnp.exp(scores - log_total).astype(jnp.bfloat16)
            mixed_ref[start:span, at : at + HEAD] = dot(soft, values_in, 1, 0).astype(jnp.bfloat16)
            log_ref[start:span, head : head + 1] = log_total


def attend_back_kernel(
    stack_ref, seg_column_ref, seg_row_ref, log_ref, grad_ref, low_ref, sums_ref
):
    length, width = grad_ref.shape
    heads = width // HEAD
    rows = length // 2
    seg_column, seg_row = seg_column_ref[...], seg_row_ref[0]
    masks = [
        allowed_block(seg_column, seg_row, block * rows, rows, (block + 1) * rows)
        for block in range(2)
    ]
    sums_ref[0] = jnp.zeros(sums_ref.shape[1:], jnp.float32)
    for head in range(heads):
        at = head * HEAD
        grad_keys, grad_values, query_sum = [], [], 0.0
        for block in range(2):
            start, span = block * rows, (block + 1) * rows
            queries = stack_ref[start:span, at : at + HEAD]
            keys_in = stack_ref[:span, width + at : width + at + HEAD]
            values_in = stack_ref[:span, 2 * width + at : 2 * width + at + HEAD]
            grad_mixed = grad_ref[start:span, at : at + HEAD]
            scores = jnp.where(masks[block], dot(queries, keys_in, 1, 1) * HEAD ** (-0.5), MASKED)
            probs = jnp.exp(scores - log_ref[start:span, head : head + 1])
            soft = probs.astype(jnp.bfloat16)
            grad_probs = dot(grad_mixed, values_in, 1, 1)
            row_dot = jnp.sum(probs * grad_probs, axis=-1, keepdims=True)
            grad_scores = (probs * (grad_probs - row_dot) * HEAD ** (-0.5)).astype(jnp.bfloat16)
            grad_queries = dot(grad_scores, keys_in, 1, 0)
            low_ref[start:span, at : at + HEAD] = grad_queries.astype(jnp.bfloat16)
            query_sum = query_sum + jnp.sum(grad_queries, axis=0, keepdims=True)
            grad_keys.append(dot(grad_scores, queries, 0, 0))
            grad_values.append(dot(soft, grad_mixed, 0, 0))
        sums_ref[0, 0:1, at : at + HEAD] = query_sum
        value_sum = 0.0
        for slot, pair in ((1, grad_keys), (2, grad_values)):
            where = slot * width + at
            upper = pair[0] + pair[1][:rows]
            lower = pair[1][rows:]
            low_ref[:rows, where : where + HEAD] = upper.astype(jnp.bfloat16)
            low_ref[rows:, where : where + HEAD] = lower.astype(jnp.bfloat16)
            if slot == 2:
                value_sum = jnp.sum(upper, axis=0, keepdims=True)
                value_sum = value_sum + jnp.sum(lower, axis=0, keepdims=True)
        sums_ref[0, 1:2, at : at + HEAD] = value_sum


def row_spec(length, width):
    return pl.BlockSpec((length, width), lambda at: (at, 0))


def attend(stack, seg_column, segments, width):
    seqs, length = segments.shape
    heads = width // HEAD
    return pl.pallas_call(
        attend_kernel,
        grid=(seqs,),
        in_specs=[
            row_spec(length, 3 * width),
            row_spec(length, 1),
            pl.BlockSpec((1, 1, length), lambda at: (at, 0, 0)),
        ],
        out_specs=[row_spec(length, width), row_spec(length, heads)],
        out_shape=[
            jax.ShapeDtypeStruct((seqs * length, width), jnp.bfloat16),
            jax.ShapeDtypeStruct((seqs * length, heads), jnp.float32),
        ],
        compiler_params=pltpu.CompilerParams(vmem_limit_bytes=40 * 2**20),
        cost_estimate=pl.CostEstimate(
            flops=8 * seqs * length * length * width, bytes_accessed=10**7, transcendentals=0
        ),
    )(stack, seg_column, segments[:, None, :])


def attend_back(stack, seg_column, segments, log_total, grad_mixed):
    seqs, length = segments.shape
    width = grad_mixed.shape[1]
    heads = width // HEAD
    low, sums = pl.pallas_call(
        attend_back_kernel,
        grid=(seqs,),
        in_specs=[
            row_spec(length, 3 * width),
            row_spec(length, 1),
            pl.BlockSpec((1, 1, length), lambda at: (at, 0, 0)),
            row_spec(length, heads),
            row_spec(length, width),
        ],
        out_specs=[
            row_spec(length, 3 * width),
            pl.BlockSpec((1, 8, width), lambda at: (at, 0, 0)),
        ],
        out_shape=[
            jax.ShapeDtypeStruct((seqs * length, 3 * width), jnp.bfloat16),
            jax.ShapeDtypeStruct((seqs, 8, width), jnp.float32),
        ],
        compiler_params=pltpu.CompilerParams(vmem_limit_bytes=40 * 2**20),
        cost_estimate=pl.CostEstimate(
            flops=20 * seqs * length * length * width, bytes_accessed=2 * 10**7, transcendentals=0
        ),
    )(stack, seg_column, segments[:, None, :], log_total, grad_mixed)
    return low, jnp.sum(sums, axis=0)[:2].reshape(-1)


def tie(*values):
    return lax.optimization_barrier(values)


class Gather:
    def __init__(self, shard, order, data_rank, data_count, bit_count):
        self.rows, self.cols = shard.shape
        self.order, self.count, self.bits = list(order), data_count, bit_count
        self.mine = [(data_rank >> (bit_count - 1 - place)) & 1 for place in range(bit_count)]
        self.done = []
        self.held = jnp.zeros(bit_shape(bit_count) + shard.shape, shard.dtype)
        self.piece = shard.reshape((1,) * bit_count + shard.shape)
        self.put(self.piece, self.mine)

    def put(self, piece, starts):
        zero = jnp.int32(0)
        self.held = lax.dynamic_update_slice(self.held, piece, list(starts) + [zero, zero])

    def step(self, steps=1):
        zero = jnp.int32(0)
        for _ in range(steps):
            bit = self.order.pop(0)
            place = self.bits - 1 - bit
            arrived = lax.ppermute(self.piece, "dp", partner_pairs(self.count, 1 << bit))
            target = [zero if at in self.done else self.mine[at] for at in range(self.bits)]
            target[place] = 1 - self.mine[place]
            self.put(arrived, target)
            self.done.append(place)
            if self.order:
                starts = [zero if at in self.done else self.mine[at] for at in range(self.bits)]
                sizes = [2 if at in self.done else 1 for at in range(self.bits)]
                self.piece = lax.dynamic_slice(
                    self.held, starts + [zero, zero], sizes + [self.rows, self.cols]
                )

    def whole(self):
        return self.held.reshape(self.count * self.rows, self.cols)


class Scatter:
    def __init__(self, term, order, data_rank, data_count, bit_count):
        self.rows, self.cols = term.shape[0] // data_count, term.shape[1]
        self.order, self.count, self.bits = list(order), data_count, bit_count
        self.mine = [(data_rank >> (bit_count - 1 - place)) & 1 for place in range(bit_count)]
        self.held = term.reshape(bit_shape(bit_count) + (self.rows, self.cols))

    def step(self, steps=1):
        for _ in range(steps):
            bit = self.order.pop(0)
            place = self.bits - 1 - bit
            away = lax.dynamic_slice_in_dim(self.held, 1 - self.mine[place], 1, place)
            kept = lax.dynamic_slice_in_dim(self.held, self.mine[place], 1, place)
            arrived = lax.ppermute(
                away.astype(jnp.bfloat16), "dp", partner_pairs(self.count, 1 << bit)
            )
            self.held = kept + arrived.astype(jnp.float32)

    def whole(self):
        self.step(len(self.order))
        return self.held.reshape(self.rows, self.cols)


def partner_pairs(count, step):
    return [(place, place ^ step) for place in range(count)]


def bit_shape(bit_count):
    return (2,) * bit_count


def total_over(flat, data_count, bit_count):
    for bit in range(bit_count):
        flat = flat + lax.ppermute(flat, "dp", partner_pairs(data_count, 1 << bit))
    return flat


def local(
    inputs,
    segments,
    norm_gains,
    norm_shifts,
    qkv_weight,
    qkv_bias,
    out_weight,
    out_biases,
    up_weight,
    up_bias,
    down_weight,
    cotangent,
):
    local_rows = inputs.shape[0]
    seq_count = segments.shape[0]
    seq_length = segments.shape[1]
    model_width = inputs.shape[1]
    tensor_rank = lax.axis_index("tensor")
    data_rank = lax.axis_index("dp")
    data_count = lax.axis_size("dp")
    bit_count = data_count.bit_length() - 1
    head_cols = qkv_weight.shape[2]
    hidden_cols = up_weight.shape[1]
    heads_here = head_cols // HEAD
    block_rows = seq_count * seq_length
    links = (data_rank, data_count, bit_count)
    rest = [bit for bit in range(bit_count - 1, 2, -1)]
    order_up = rest + [2, 1, 0]
    order_down = rest + [2, 0, 1]
    order_turn = rest + [1, 0, 2]
    orders = (order_turn, order_up, order_down)

    qkv_parts = [Gather(qkv_weight[at], orders[at], *links) for at in range(3)]
    out_part = Gather(out_weight.T, order_turn, *links)
    up_part = Gather(up_weight, order_up, *links)
    down_part = Gather(down_weight.T, order_down, *links)
    later = (out_part, up_part, down_part)
    early = bit_count - 2
    for part in qkv_parts:
        part.step(bit_count - 1)
    for part in later:
        part.step(early)
    tied = tie(*[part.piece for part in qkv_parts], *[part.piece for part in later])
    for at in range(3):
        qkv_parts[at].piece, later[at].piece = tied[at], tied[3 + at]
    for part in qkv_parts:
        part.step()
    for part in later:
        part.step()

    def spread(row_block):
        return lax.all_gather(row_block, "tensor", axis=0, tiled=True)

    def collect(left_rows, right_matrix, dims):
        def term(rank):
            part = lax.dynamic_slice_in_dim(left_rows, rank * local_rows, local_rows, 0)
            return lax.dot_general(
                part, right_matrix, (dims, ((), ())), preferred_element_type=jnp.float32
            )

        arrived = lax.ppermute(term(1 - tensor_rank), "tensor", [(0, 1), (1, 0)])
        return term(tensor_rank) + arrived

    plain, turned = ((1,), (0,)), ((1,), (1,))
    stream = inputs.astype(jnp.float32)
    normed, unit_one, inverse_one = normalize(stream, norm_gains[0], norm_shifts[0])
    hidden_one = spread(normed.astype(jnp.bfloat16))
    grad_stream = cotangent.astype(jnp.float32)
    grad_rows = spread(cotangent)
    zeros = jnp.zeros((head_cols,), jnp.float32)
    biases = (qkv_bias[0], zeros, qkv_bias[1])
    qkv_full = [part.whole() for part in qkv_parts]
    stack_rows = jnp.concatenate(
        [
            (
                jnp.dot(hidden_one, qkv_full[at], preferred_element_type=jnp.float32) + biases[at]
            ).astype(jnp.bfloat16)
            for at in range(3)
        ],
        axis=1,
    )
    tied = tie(stack_rows, *[part.piece for part in later])
    stack_rows = tied[0]
    for part, piece in zip(later, tied[1:]):
        part.piece = piece
        part.step()
    out_full, up_full, down_full = [part.whole() for part in later]
    seg_column = segments.reshape(block_rows, 1)
    mixed_rows, log_total = attend(stack_rows, seg_column, segments, head_cols)
    middle = stream + collect(mixed_rows, out_full, turned) + out_biases[0]
    normed_two, unit_two, inverse_two = normalize(middle, norm_gains[1], norm_shifts[1])
    hidden_two = spread(normed_two.astype(jnp.bfloat16))
    before = jnp.dot(hidden_two, up_full, preferred_element_type=jnp.float32) + up_bias
    activated = gaussian_unit(before).astype(jnp.bfloat16)
    down_turned = jnp.einsum("rd,rj->dj", grad_rows, activated, preferred_element_type=jnp.float32)
    down_sum = Scatter(down_turned, order_down[::-1], *links)
    down_sum.step()
    grad_active = jnp.dot(grad_rows, down_full, preferred_element_type=jnp.float32)
    grad_before = jax.vjp(gaussian_unit, before)[1](grad_active)[0]
    before_low = grad_before.astype(jnp.bfloat16)
    grad_up = jnp.einsum("rd,rj->dj", hidden_two, before_low, preferred_element_type=jnp.float32)
    up_sum = Scatter(grad_up, order_up[::-1], *links)
    up_sum.step()
    grad_hidden_two = collect(before_low, up_full, turned)
    grad_middle = grad_stream + normalize_back(
        grad_hidden_two, unit_two, inverse_two, norm_gains[1]
    )
    middle_rows = spread(grad_middle.astype(jnp.bfloat16))
    out_turned = jnp.einsum(
        "rd,rj->dj", middle_rows, mixed_rows, preferred_element_type=jnp.float32
    )
    out_sum = Scatter(out_turned, order_turn[::-1], *links)
    out_sum.step()
    grad_mixed = jnp.dot(middle_rows, out_full, preferred_element_type=jnp.float32).astype(
        jnp.bfloat16
    )
    grad_mixed, down_sum.held = tie(grad_mixed, down_sum.held)
    down_sum.step()
    result = (middle + collect(activated, down_full, turned) + out_biases[1]).astype(jnp.bfloat16)
    stack_low, bias_sums = attend_back(stack_rows, seg_column, segments, log_total, grad_mixed)
    stack_low, up_sum.held, out_sum.held = tie(stack_low, up_sum.held, out_sum.held)
    up_sum.step()
    out_sum.step()
    qkv_sums = []
    for at in range(3):
        term = dot(hidden_one, stack_low[:, at * head_cols : (at + 1) * head_cols], 0, 0)
        qkv_sums.append(Scatter(term, orders[at][::-1], *links))
        qkv_sums[at].step()
    grad_hidden_one = collect(stack_low, jnp.concatenate(qkv_full, axis=1), turned)
    grad_input = grad_middle + normalize_back(grad_hidden_one, unit_one, inverse_one, norm_gains[0])
    vectors = jnp.concatenate(
        [
            jnp.sum(grad_hidden_one * unit_one, axis=0),
            jnp.sum(grad_hidden_two * unit_two, axis=0),
            jnp.sum(grad_hidden_one, axis=0),
            jnp.sum(grad_hidden_two, axis=0),
            jnp.sum(grad_middle, axis=0),
            jnp.sum(grad_stream, axis=0),
        ]
    )
    vectors = vectors + lax.ppermute(vectors, "tensor", [(0, 1), (1, 0)])
    flat = jnp.concatenate(
        [
            vectors,
            bias_sums,
            jnp.sum(grad_before, axis=0),
        ]
    )
    flat = total_over(flat, data_count, bit_count)
    qkv_summed = jnp.stack([part.whole() for part in qkv_sums])
    out_summed, down_summed = out_sum.whole().T, down_sum.whole().T
    up_summed = up_sum.whole()
    vector_total = flat[: 6 * model_width].reshape(6, model_width)
    rest_total = flat[6 * model_width :]
    qkv_bias_grad = rest_total[: 2 * head_cols].reshape(2, head_cols)
    up_bias_grad = rest_total[2 * head_cols :]
    return (
        result,
        grad_input,
        vector_total[0:2],
        vector_total[2:4],
        qkv_summed,
        qkv_bias_grad,
        out_summed,
        vector_total[4:6],
        up_summed,
        up_bias_grad,
        down_summed,
    )


def solution(mesh):
    in_specs = (
        P(("dp", "tensor"), None),
        P("dp", None),
        P(),
        P(),
        P(None, "dp", "tensor"),
        P(None, "tensor"),
        P("tensor", "dp"),
        P(),
        P("dp", "tensor"),
        P("tensor"),
        P("tensor", "dp"),
        P(("dp", "tensor"), None),
    )
    out_specs = (
        P(("dp", "tensor"), None),
        P(("dp", "tensor"), None),
        P(),
        P(),
        P(None, "dp", "tensor"),
        P(None, "tensor"),
        P("tensor", "dp"),
        P(),
        P("dp", "tensor"),
        P("tensor"),
        P("tensor", "dp"),
    )
    return jax.shard_map(local, mesh=mesh, in_specs=in_specs, out_specs=out_specs, check_vma=False)
```

```python
import jax
import jax.numpy as jnp
from jax import lax
from jax.experimental import pallas as pl
from jax.experimental.pallas import tpu as pltpu
from jax.sharding import PartitionSpec as P

HEAD = 64


EPSILON = 1e-05
MASKED = -1e30


def normalize(row_block, gain, shift):
    center = jnp.mean(row_block, axis=-1, keepdims=True)
    centered = row_block - center
    spread = jnp.mean(centered * centered, axis=-1, keepdims=True)
    inverse = lax.rsqrt(spread + EPSILON)
    unit_rows = centered * inverse
    return (unit_rows * gain + shift, unit_rows, inverse)


def normalize_back(grad_rows, unit_rows, inverse, gain):
    scaled = grad_rows * gain
    first_mean = jnp.mean(scaled, axis=-1, keepdims=True)
    second_mean = jnp.mean(scaled * unit_rows, axis=-1, keepdims=True)
    return inverse * (scaled - first_mean - unit_rows * second_mean)


def gaussian_unit(values_in):
    return jax.nn.gelu(values_in, approximate=True)


def dot(left, right, left_dim, right_dim):
    return lax.dot_general(
        left, right, (((left_dim,), (right_dim,)), ((), ())), preferred_element_type=jnp.float32
    )


def allowed_block(seg_column, seg_row, start, rows, span):
    row_at = lax.broadcasted_iota(jnp.int32, (rows, span), 0) + start
    col_at = lax.broadcasted_iota(jnp.int32, (rows, span), 1)
    same = seg_column[start : start + rows, :] == seg_row[:, :span]
    return same & (row_at >= col_at)


def attend_kernel(stack_ref, seg_column_ref, seg_row_ref, mixed_ref, log_ref):
    length, width = mixed_ref.shape
    heads = width // HEAD
    rows = length // 2
    seg_column, seg_row = seg_column_ref[...], seg_row_ref[0]
    for block in range(2):
        start, span = block * rows, (block + 1) * rows
        allowed = allowed_block(seg_column, seg_row, start, rows, span)
        for head in range(heads):
            at = head * HEAD
            queries = stack_ref[start:span, at : at + HEAD]
            keys_in = stack_ref[:span, width + at : width + at + HEAD]
            values_in = stack_ref[:span, 2 * width + at : 2 * width + at + HEAD]
            scores = jnp.where(allowed, dot(queries, keys_in, 1, 1) * HEAD ** (-0.5), MASKED)
            top = jnp.max(scores, axis=-1, keepdims=True)
            total = jnp.sum(jnp.exp(scores - top), axis=-1, keepdims=True)
            log_total = top + jnp.log(total)
            soft = jnp.exp(scores - log_total).astype(jnp.bfloat16)
            mixed_ref[start:span, at : at + HEAD] = dot(soft, values_in, 1, 0).astype(jnp.bfloat16)
            log_ref[start:span, head : head + 1] = log_total


def attend_back_kernel(
    stack_ref, seg_column_ref, seg_row_ref, log_ref, grad_ref, low_ref, sums_ref
):
    length, width = grad_ref.shape
    heads = width // HEAD
    rows = length // 2
    seg_column, seg_row = seg_column_ref[...], seg_row_ref[0]
    masks = [
        allowed_block(seg_column, seg_row, block * rows, rows, (block + 1) * rows)
        for block in range(2)
    ]
    sums_ref[0] = jnp.zeros(sums_ref.shape[1:], jnp.float32)
    for head in range(heads):
        at = head * HEAD
        grad_keys, grad_values, query_sum = [], [], 0.0
        for block in range(2):
            start, span = block * rows, (block + 1) * rows
            queries = stack_ref[start:span, at : at + HEAD]
            keys_in = stack_ref[:span, width + at : width + at + HEAD]
            values_in = stack_ref[:span, 2 * width + at : 2 * width + at + HEAD]
            grad_mixed = grad_ref[start:span, at : at + HEAD]
            scores = jnp.where(masks[block], dot(queries, keys_in, 1, 1) * HEAD ** (-0.5), MASKED)
            probs = jnp.exp(scores - log_ref[start:span, head : head + 1])
            soft = probs.astype(jnp.bfloat16)
            grad_probs = dot(grad_mixed, values_in, 1, 1)
            row_dot = jnp.sum(probs * grad_probs, axis=-1, keepdims=True)
            grad_scores = (probs * (grad_probs - row_dot) * HEAD ** (-0.5)).astype(jnp.bfloat16)
            grad_queries = dot(grad_scores, keys_in, 1, 0)
            low_ref[start:span, at : at + HEAD] = grad_queries.astype(jnp.bfloat16)
            query_sum = query_sum + jnp.sum(grad_queries, axis=0, keepdims=True)
            grad_keys.append(dot(grad_scores, queries, 0, 0))
            grad_values.append(dot(soft, grad_mixed, 0, 0))
        sums_ref[0, 0:1, at : at + HEAD] = query_sum
        value_sum = 0.0
        for slot, pair in ((1, grad_keys), (2, grad_values)):
            where = slot * width + at
            upper = pair[0] + pair[1][:rows]
            lower = pair[1][rows:]
            low_ref[:rows, where : where + HEAD] = upper.astype(jnp.bfloat16)
            low_ref[rows:, where : where + HEAD] = lower.astype(jnp.bfloat16)
            if slot == 2:
                value_sum = jnp.sum(upper, axis=0, keepdims=True)
                value_sum = value_sum + jnp.sum(lower, axis=0, keepdims=True)
        sums_ref[0, 1:2, at : at + HEAD] = value_sum


def row_spec(length, width):
    return pl.BlockSpec((length, width), lambda at: (at, 0))


def attend(stack, seg_column, segments, width):
    seqs, length = segments.shape
    heads = width // HEAD
    return pl.pallas_call(
        attend_kernel,
        grid=(seqs,),
        in_specs=[
            row_spec(length, 3 * width),
            row_spec(length, 1),
            pl.BlockSpec((1, 1, length), lambda at: (at, 0, 0)),
        ],
        out_specs=[row_spec(length, width), row_spec(length, heads)],
        out_shape=[
            jax.ShapeDtypeStruct((seqs * length, width), jnp.bfloat16),
            jax.ShapeDtypeStruct((seqs * length, heads), jnp.float32),
        ],
        compiler_params=pltpu.CompilerParams(vmem_limit_bytes=40 * 2**20),
        cost_estimate=pl.CostEstimate(
            flops=8 * seqs * length * length * width, bytes_accessed=10**7, transcendentals=0
        ),
    )(stack, seg_column, segments[:, None, :])


def attend_back(stack, seg_column, segments, log_total, grad_mixed):
    seqs, length = segments.shape
    width = grad_mixed.shape[1]
    heads = width // HEAD
    low, sums = pl.pallas_call(
        attend_back_kernel,
        grid=(seqs,),
        in_specs=[
            row_spec(length, 3 * width),
            row_spec(length, 1),
            pl.BlockSpec((1, 1, length), lambda at: (at, 0, 0)),
            row_spec(length, heads),
            row_spec(length, width),
        ],
        out_specs=[
            row_spec(length, 3 * width),
            pl.BlockSpec((1, 8, width), lambda at: (at, 0, 0)),
        ],
        out_shape=[
            jax.ShapeDtypeStruct((seqs * length, 3 * width), jnp.bfloat16),
            jax.ShapeDtypeStruct((seqs, 8, width), jnp.float32),
        ],
        compiler_params=pltpu.CompilerParams(vmem_limit_bytes=40 * 2**20),
        cost_estimate=pl.CostEstimate(
            flops=20 * seqs * length * length * width, bytes_accessed=2 * 10**7, transcendentals=0
        ),
    )(stack, seg_column, segments[:, None, :], log_total, grad_mixed)
    return low, jnp.sum(sums, axis=0)[:2].reshape(-1)


def tie(*values):
    return lax.optimization_barrier(values)


def partner_pairs(count, step):
    return [(place, place ^ step) for place in range(count)]


def digits_of(rank, count):
    sizes, strides, stride = [], [], 1
    while stride < count:
        size = min(4, count // stride)
        sizes.insert(0, size)
        strides.insert(0, stride)
        stride *= size
    return sizes, strides, [(rank // at) % size for at, size in zip(strides, sizes)]


def gather_round(held, place, digits, count):
    sizes, strides, mine = digits
    zero = jnp.int32(0)
    shape = held.shape[:place] + (sizes[place],) + held.shape[place:]
    whole = jnp.zeros(shape, held.dtype)
    for other in range(sizes[place]):
        arrived = held
        if other:
            arrived = lax.ppermute(held, "dp", partner_pairs(count, other * strides[place]))
        starts = [zero] * len(shape)
        starts[place] = mine[place] ^ other
        whole = lax.dynamic_update_slice(whole, jnp.expand_dims(arrived, place), starts)
    return whole


def gather_rows(shard, digits, count):
    for place in range(len(digits[0])):
        shard = gather_round(shard, place, digits, count)
    return shard.reshape(-1, shard.shape[-1])


def split_rows(term, digits, count):
    return term.reshape(tuple(digits[0]) + (term.shape[0] // count, term.shape[1]))


def scatter_round(terms, place, digits, count):
    sizes, strides, mine = digits

    def block(other):
        cut = [lax.dynamic_index_in_dim(t, mine[place] ^ other, place, False) for t in terms]
        return cut

    arrivals = []
    for other in range(1, sizes[place]):
        away = jnp.concatenate([cut.astype(jnp.bfloat16) for cut in block(other)], axis=-1)
        arrivals.append(lax.ppermute(away, "dp", partner_pairs(count, other * strides[place])))
    total = jnp.concatenate(block(0), axis=-1)
    for arrived in arrivals:
        total = total + arrived.astype(jnp.float32)
    return [total]


def total_over(flat, digits, count):
    for size, stride in zip(digits[0], digits[1]):
        got = [lax.ppermute(flat, "dp", partner_pairs(count, at * stride)) for at in range(1, size)]
        flat = flat + got[0]
        if size == 4:
            flat = flat + (got[1] + got[2])
    return flat


def local(
    inputs,
    segments,
    norm_gains,
    norm_shifts,
    qkv_weight,
    qkv_bias,
    out_weight,
    out_biases,
    up_weight,
    up_bias,
    down_weight,
    cotangent,
):
    local_rows = inputs.shape[0]
    seq_count = segments.shape[0]
    seq_length = segments.shape[1]
    model_width = inputs.shape[1]
    tensor_rank = lax.axis_index("tensor")
    data_rank = lax.axis_index("dp")
    data_count = lax.axis_size("dp")
    head_cols = qkv_weight.shape[2]
    hidden_cols = up_weight.shape[1]
    heads_here = head_cols // HEAD
    block_rows = seq_count * seq_length
    digits = digits_of(data_rank, data_count)
    rounds = range(len(digits[0]) - 1, -1, -1)

    first = jnp.concatenate([qkv_weight[0], qkv_weight[1], qkv_weight[2], out_weight.T], axis=1)
    first_full = gather_rows(first, digits, data_count)
    up_full = gather_rows(up_weight, digits, data_count)
    down_full = gather_rows(down_weight.T, digits, data_count)
    qkv_full = first_full[:, : 3 * head_cols]
    out_full = first_full[:, 3 * head_cols :]

    def spread(row_block):
        return lax.all_gather(row_block, "tensor", axis=0, tiled=True)

    def collect(left_rows, right_matrix, dims):
        def term(rank):
            part = lax.dynamic_slice_in_dim(left_rows, rank * local_rows, local_rows, 0)
            return lax.dot_general(
                part, right_matrix, (dims, ((), ())), preferred_element_type=jnp.float32
            )

        arrived = lax.ppermute(term(1 - tensor_rank), "tensor", [(0, 1), (1, 0)])
        return term(tensor_rank) + arrived

    plain, turned = ((1,), (0,)), ((1,), (1,))
    stream = inputs.astype(jnp.float32)
    normed, unit_one, inverse_one = normalize(stream, norm_gains[0], norm_shifts[0])
    hidden_one = spread(normed.astype(jnp.bfloat16))
    grad_stream = cotangent.astype(jnp.float32)
    grad_rows = spread(cotangent)
    zeros = jnp.zeros((head_cols,), jnp.float32)
    stack_bias = jnp.concatenate([qkv_bias[0], zeros, qkv_bias[1]])
    stack_rows = jnp.dot(hidden_one, qkv_full, preferred_element_type=jnp.float32) + stack_bias
    stack_rows = stack_rows.astype(jnp.bfloat16)
    seg_column = segments.reshape(block_rows, 1)
    mixed_rows, log_total = attend(stack_rows, seg_column, segments, head_cols)
    middle = stream + collect(mixed_rows, out_full, turned) + out_biases[0]
    normed_two, unit_two, inverse_two = normalize(middle, norm_gains[1], norm_shifts[1])
    hidden_two = spread(normed_two.astype(jnp.bfloat16))
    before = jnp.dot(hidden_two, up_full, preferred_element_type=jnp.float32) + up_bias
    activated = gaussian_unit(before).astype(jnp.bfloat16)
    down_turned = jnp.einsum("rd,rj->dj", grad_rows, activated, preferred_element_type=jnp.float32)
    grad_active = jnp.dot(grad_rows, down_full, preferred_element_type=jnp.float32)
    grad_before = jax.vjp(gaussian_unit, before)[1](grad_active)[0]
    before_low = grad_before.astype(jnp.bfloat16)
    grad_up = jnp.einsum("rd,rj->dj", hidden_two, before_low, preferred_element_type=jnp.float32)
    wide = scatter_round(
        [split_rows(grad_up, digits, data_count), split_rows(down_turned, digits, data_count)],
        rounds[0],
        digits,
        data_count,
    )
    grad_hidden_two = collect(before_low, up_full, turned)
    grad_middle = grad_stream + normalize_back(
        grad_hidden_two, unit_two, inverse_two, norm_gains[1]
    )
    middle_rows = spread(grad_middle.astype(jnp.bfloat16))
    out_turned = jnp.einsum(
        "rd,rj->dj", middle_rows, mixed_rows, preferred_element_type=jnp.float32
    )
    grad_mixed = jnp.dot(middle_rows, out_full, preferred_element_type=jnp.float32).astype(
        jnp.bfloat16
    )
    result = (middle + collect(activated, down_full, turned) + out_biases[1]).astype(jnp.bfloat16)
    stack_low, bias_sums = attend_back(stack_rows, seg_column, segments, log_total, grad_mixed)
    stack_low, wide[0] = tie(stack_low, wide[0])
    grad_qkv = dot(hidden_one, stack_low, 0, 0)
    slim = scatter_round(
        [split_rows(grad_qkv, digits, data_count), split_rows(out_turned, digits, data_count)],
        rounds[0],
        digits,
        data_count,
    )
    for place in rounds[1:]:
        wide = scatter_round(wide, place, digits, data_count)
        slim = scatter_round(slim, place, digits, data_count)
    grad_hidden_one = collect(stack_low, qkv_full, turned)
    grad_input = grad_middle + normalize_back(grad_hidden_one, unit_one, inverse_one, norm_gains[0])
    vectors = jnp.concatenate(
        [
            jnp.sum(grad_hidden_one * unit_one, axis=0),
            jnp.sum(grad_hidden_two * unit_two, axis=0),
            jnp.sum(grad_hidden_one, axis=0),
            jnp.sum(grad_hidden_two, axis=0),
            jnp.sum(grad_middle, axis=0),
            jnp.sum(grad_stream, axis=0),
        ]
    )
    vectors = vectors + lax.ppermute(vectors, "tensor", [(0, 1), (1, 0)])
    flat = jnp.concatenate(
        [
            vectors,
            bias_sums,
            jnp.sum(grad_before, axis=0),
        ]
    )
    flat = total_over(flat, digits, data_count)
    qkv_summed = jnp.stack([slim[0][:, at * head_cols : (at + 1) * head_cols] for at in range(3)])
    out_summed = slim[0][:, 3 * head_cols :].T
    up_summed = wide[0][:, :hidden_cols]
    down_summed = wide[0][:, hidden_cols:].T
    vector_total = flat[: 6 * model_width].reshape(6, model_width)
    rest_total = flat[6 * model_width :]
    qkv_bias_grad = rest_total[: 2 * head_cols].reshape(2, head_cols)
    up_bias_grad = rest_total[2 * head_cols :]
    return (
        result,
        grad_input,
        vector_total[0:2],
        vector_total[2:4],
        qkv_summed,
        qkv_bias_grad,
        out_summed,
        vector_total[4:6],
        up_summed,
        up_bias_grad,
        down_summed,
    )


def solution(mesh):
    in_specs = (
        P(("dp", "tensor"), None),
        P("dp", None),
        P(),
        P(),
        P(None, "dp", "tensor"),
        P(None, "tensor"),
        P("tensor", "dp"),
        P(),
        P("dp", "tensor"),
        P("tensor"),
        P("tensor", "dp"),
        P(("dp", "tensor"), None),
    )
    out_specs = (
        P(("dp", "tensor"), None),
        P(("dp", "tensor"), None),
        P(),
        P(),
        P(None, "dp", "tensor"),
        P(None, "tensor"),
        P("tensor", "dp"),
        P(),
        P("dp", "tensor"),
        P("tensor"),
        P("tensor", "dp"),
    )
    return jax.shard_map(local, mesh=mesh, in_specs=in_specs, out_specs=out_specs, check_vma=False)
```
